512 devices in a mesh: corpus: 128 (over z, y, core), query: 4 (over x).
Axes of the slice: x: 4, y: 4, z: 16, core: 2. Of those that a mesh axis runs over, the one named last changes fastest.
Arguments:
- prefixes: bfloat16 [32768, 256], P(('corpus', 'query')), as said below
- tails: bfloat16 [32768, 2816], P('corpus'), as said below
- queries_now: bfloat16 [32768, 256], P(('corpus', 'query')), as said below
- queries_prev: bfloat16 [512, 3072], P(('corpus', 'query')), may hold values from -6 to 6
- candidates: int32 [512, 100], P(('corpus', 'query')), may hold values from 0 to 32767, as said below
- lse_prev: float32 [512], P(('corpus', 'query')), may hold values from 9 to 14
Outputs:
- lse_now: float32 [32768], P(('corpus', 'query'))
- rerank: float32 [512, 100], P(('corpus', 'query'))
The draws below stay inside these ranges and needn't reach their ends.
Inputs may be any that keep to these rules, and one draw needn't show every extreme that they name: `prefixes`: prefix coordinates of the passage embeddings. `tails`: remaining coordinates of the passage embeddings. `queries_now`: query prefixes. `candidates`: passage j belongs to corpus index j // 256. Among the 100 ids of one device's queries, at most 2 belong to one corpus index, and exactly 2 to some corpus index. Ids may repeat.
All inputs are finite; a program needn't handle non-finite values.
Results may differ from the reference program's by a relative error of at most 0.0003.
Values may be sent and summed in bfloat16 or wider, within the bound.
No kernel may reach another device: no remote copies, remote signals or barrier semaphores. Data moves between devices by JAX's collectives and lax.ppermute only.
A program may use at most 64 MiB of HBM per device.

```python
import math
import jax
import jax.numpy as jnp
from jax import lax

F = 3072
P_SIZE = 256
PASS_DEV = 256
PREV_DEV = 1
CAND = 100
PASSAGES = 32768
NOW_QUERIES = 32768
PREV_QUERIES = 512
CAP = 2
N_CORPUS = 128
N_QUERY = 4


def corpus_parts(key, low_scale, high_scale):
    key_prefix, key_tail, key_rows, key_columns = jax.random.split(key, 4)
    position = jnp.arange(PASSAGES, dtype=jnp.float32) / PASSAGES
    row_scale = jnp.exp(jax.random.uniform(key_rows, (PASSAGES,), jnp.float32, math.log(low_scale), math.log(high_scale))) * jnp.sqrt(1.0 + 2.0 * position)
    column_scale = jnp.exp(jax.random.uniform(key_columns, (F,), jnp.float32, math.log(0.5), math.log(2.0)))
    prefix_part = jax.random.normal(key_prefix, (PASSAGES, P_SIZE), jnp.float32) * row_scale[:, None] * column_scale[None, :P_SIZE]
    return (prefix_part, key_tail, row_scale, column_scale)


def draw_prefixes(key, part):
    prefix_part, key_tail, row_scale, column_scale = corpus_parts(key, 0.5, 2.0)
    return prefix_part.astype(jnp.bfloat16)


def draw_tails(key, part):
    prefix_part, key_tail, row_scale, column_scale = corpus_parts(key, 0.5, 2.0)
    tail_part = jax.random.normal(key_tail, (PASSAGES, F - P_SIZE), jnp.float32) * row_scale[:, None] * column_scale[None, P_SIZE:]
    return tail_part.astype(jnp.bfloat16)


def draw_queries_now(key, part):
    key = jax.random.fold_in(key, 5)
    key_base = jax.random.fold_in(key, 0)
    values = jax.random.normal(key_base, (NOW_QUERIES, P_SIZE), jnp.float32)
    return values.astype(jnp.bfloat16)


def draw_candidates(key, part):
    key = jax.random.fold_in(key, 7)
    key_hot, key_order, key_spread, key_local = jax.random.split(key, 4)
    device_count = N_CORPUS * N_QUERY
    slot_count = PREV_DEV * CAND
    hot_owner = jax.random.randint(key_hot, (N_QUERY,), 0, N_CORPUS)
    hot_device = hot_owner[jnp.arange(device_count) % N_QUERY]
    order_keys = jax.random.randint(key_order, (device_count, slot_count), 0, 1 << 20) * slot_count + jnp.arange(slot_count)[None, :]
    assigned = jnp.argsort(order_keys, axis=1).astype(jnp.int32)
    other_keys = jax.random.randint(key_spread, (device_count, N_CORPUS - 1), 0, 1 << 20) * (N_CORPUS - 1) + jnp.arange(N_CORPUS - 1)[None, :]
    others = jnp.argsort(other_keys, axis=1).astype(jnp.int32)
    wrapped = jnp.maximum(assigned - CAP, 0) % (N_CORPUS - 1)
    other_owner = jnp.take_along_axis(others, wrapped, axis=1)
    owners = jnp.where(assigned < CAP, hot_device[:, None], (hot_device[:, None] + 1 + other_owner) % N_CORPUS)
    local_rows = jax.random.randint(key_local, (device_count, slot_count), 0, PASS_DEV)
    return (owners * PASS_DEV + local_rows).reshape(device_count * PREV_DEV, CAND).astype(jnp.int32)


def steps_of(key, extent, cuts, least, high):
    def one(dim, parts):
        steps = jax.random.uniform(jax.random.fold_in(jax.random.fold_in(key, 6), dim), (parts,), jnp.float32, least / len(cuts), high / len(cuts))
        return jnp.repeat(jnp.exp(steps), extent[dim] // parts).reshape((-1,) + (1,) * (len(extent) - dim - 1))

    level = one(*cuts[0])
    for cut in cuts[1:]:
        level = level * one(*cut)
    return level


def gaussian(stream_key, extent, width, limit, shards=(), kind=jnp.bfloat16):
    loudness = steps_of(stream_key, extent, shards, -0.22, 0.18) if shards else 1.0
    drawn = jax.random.normal(stream_key, extent, jnp.float32) * width * loudness
    return jnp.minimum(jnp.maximum(drawn, -limit), limit).astype(kind)


def setup_inputs(seed: int = 0) -> dict:
    seeds = jax.random.split(jax.random.key(seed), 7)
    return {
        "prefixes": draw_prefixes(jax.random.fold_in(seeds[6], 71), 0),
        "tails": draw_tails(jax.random.fold_in(seeds[6], 71), 0),
        "queries_now": draw_queries_now(jax.random.fold_in(seeds[6], 71), 0),
        "queries_prev": gaussian(seeds[3], (PREV_QUERIES, F), 1.0, 6.0, ((0, 512),)),
        "candidates": draw_candidates(jax.random.fold_in(seeds[6], 71), 0),
        "lse_prev": jnp.clip(9.0 + 5.0 * jax.random.uniform(seeds[5], (PREV_QUERIES,), jnp.float32) ** steps_of(seeds[5], (PREV_QUERIES,), ((0, 512),), -0.2, 0.2), 9.0, 14.0),
    }


def reference(prefixes, tails, queries_now, queries_prev, candidates, lse_prev):
    now_count = queries_now.shape[0]
    block_size = math.gcd(now_count, 1024)

    def score_block(block_rows):
        scores = jnp.dot(block_rows, prefixes.T, preferred_element_type=jnp.float32) * (P_SIZE ** -0.5)
        return jax.nn.logsumexp(scores, axis=1)

    lse_now = lax.map(score_block, queries_now.reshape(now_count // block_size, block_size, P_SIZE)).reshape(-1)
    prev_count = queries_prev.shape[0]
    rerank_size = math.gcd(prev_count, 16)

    def rerank_block(pair_args):
        block_queries, block_ids = pair_args
        head_rows = prefixes[block_ids].astype(jnp.float32)
        tail_rows = tails[block_ids].astype(jnp.float32)
        query_full = block_queries.astype(jnp.float32)
        head_part = jnp.einsum("qf,qcf->qc", query_full[:, :P_SIZE], head_rows)
        tail_part = jnp.einsum("qf,qcf->qc", query_full[:, P_SIZE:], tail_rows)
        return head_part + tail_part

    full_scores = lax.map(rerank_block, (queries_prev.reshape(prev_count // rerank_size, rerank_size, F), candidates.reshape(prev_count // rerank_size, rerank_size, CAND)))
    full_scores = full_scores.reshape(prev_count, CAND)
    rerank = full_scores * (F ** -0.5) - lse_prev[:, None]
    return lse_now, rerank
```

```python
import jax
import jax.numpy as jnp
from jax import lax
from jax.experimental import pallas as pl
from jax.experimental.pallas import tpu as pltpu
from jax.sharding import Mesh, PartitionSpec as P

ALL = ("z", "y", "core", "x")
PLANE = ("y", "core", "x")
BACK = ("core", "y", "z")
LOG2E = 1.4426950408889634


def partial_lse(scale, queries_ref, passages_ref, out_ref, scores):
    groups, rows = queries_ref.shape[0], out_ref.shape[1] // queries_ref.shape[0]
    width = passages_ref.shape[1]
    block = queries_ref[:, :rows, :].reshape(groups * rows, width)
    count, step = passages_ref.shape[0], 256
    top = None
    for start in range(0, count, step):
        part = lax.dot_general(
            passages_ref[start : start + step, :],
            block,
            (((1,), (1,)), ((), ())),
            preferred_element_type=jnp.float32,
        )
        scores[start : start + step, :] = part
        high = jnp.max(part.reshape(step // 8, 8, groups * rows), axis=0)
        top = high if top is None else jnp.maximum(top, high)
    peak = jnp.max(top, axis=0, keepdims=True)
    total = None
    for start in range(0, count, step):
        part = jnp.exp2((scores[start : start + step, :] - peak) * (scale * LOG2E))
        added = jnp.sum(part.reshape(step // 8, 8, groups * rows), axis=0)
        total = added if total is None else total + added
    out_ref[...] = peak * scale + jnp.log(jnp.sum(total, axis=0, keepdims=True))


def passage_scores(place_ref, asked_ref, prefixes_ref, tails_ref, out_ref):
    rows, head = tails_ref.shape[0], prefixes_ref.shape[1]
    start = pl.multiple_of(place_ref[0] * rows, rows)
    dims = (((1,), (1,)), ((), ()))
    out_ref[...] = lax.dot_general(
        asked_ref[:, :head], prefixes_ref[pl.ds(start, rows), :], dims, preferred_element_type=jnp.float32
    ) + lax.dot_general(asked_ref[:, head:], tails_ref[...], dims, preferred_element_type=jnp.float32)


def finish(scale, rows, own_ref, row_ref, column_ref, back_ref, prev_ref, lse_ref, rerank_ref, picked):
    count = rerank_ref.shape[1]
    width = back_ref.shape[1]
    depth = 16
    start = pl.multiple_of(own_ref[0] * depth, depth)
    parts = back_ref[pl.ds(start, depth), rows:]
    peak = jnp.max(parts, axis=0, keepdims=True)
    lse_ref[...] = peak + jnp.log(jnp.sum(jnp.exp(parts - peak), axis=0, keepdims=True))
    lanes = lax.broadcasted_iota(jnp.int32, (1, rows), 1)
    picked[...] = jnp.zeros_like(picked)
    for k in range(count):
        row = back_ref[pl.ds(row_ref[k], 1), :rows]
        row = jnp.where(lanes == column_ref[k], row, 0.0)
        picked[k : k + 1, :] = row[:, :128] + row[:, 128:]
    values = jnp.sum(picked[...].T, axis=0, keepdims=True)
    rerank_ref[...] = values[:, :count] * scale - prev_ref[0]


def local(prefixes, tails, queries_now, queries_prev, candidates, lse_prev):
    vmem, smem = pl.BlockSpec(memory_space=pltpu.VMEM), pl.BlockSpec(memory_space=pltpu.SMEM)
    depth = lax.axis_size("z")
    own_rows, head = queries_now.shape
    shard_rows = tails.shape[0]
    full_width = queries_prev.shape[1]
    plane = lax.axis_size("y") * lax.axis_size("core")

    passages = lax.all_to_all(
        jnp.broadcast_to(prefixes[None], (plane * lax.axis_size("x"),) + prefixes.shape),
        PLANE, 0, 0, tiled=True,
    ).reshape(-1, head)

    extra = full_width // head
    sent = jnp.concatenate([queries_now, queries_prev.reshape(extra, head), jnp.zeros((16 - extra, head), queries_now.dtype)])
    column = lax.all_gather(sent, "z")
    asked = column[:, own_rows : own_rows + extra].reshape(depth, full_width)

    asked = lax.all_to_all(
        jnp.broadcast_to(asked[None], (lax.axis_size("y"),) + asked.shape), "y", 0, 0, tiled=True
    ).reshape(-1, full_width)
    asked = lax.all_gather(asked, "core", tiled=True)

    step = 4
    lse_parts = pl.pallas_call(
        lambda *refs: partial_lse(head**-0.5, *refs),
        grid=(depth // step,),
        in_specs=[
            pl.BlockSpec((step,) + column.shape[1:], lambda i: (i, 0, 0)),
            pl.BlockSpec(passages.shape, lambda i: (0, 0)),
        ],
        out_specs=pl.BlockSpec((1, step * own_rows), lambda i: (0, i)),
        out_shape=jax.ShapeDtypeStruct((1, depth * own_rows), jnp.float32),
        scratch_shapes=[pltpu.VMEM((passages.shape[0], step * own_rows), jnp.float32)],
        compiler_params=pltpu.CompilerParams(vmem_limit_bytes=32 * 2**20),
        cost_estimate=pl.CostEstimate(flops=2 * 2**28, bytes_accessed=2 * 2**20, transcendentals=2**21),
        name="partial_lse",
    )(column, passages)

    place = lax.axis_index("y") * lax.axis_size("core") + lax.axis_index("core")
    scores = pl.pallas_call(
        passage_scores,
        in_specs=[smem, vmem, vmem, vmem],
        out_specs=vmem,
        out_shape=jax.ShapeDtypeStruct((plane * depth, shard_rows), jnp.float32),
        compiler_params=pltpu.CompilerParams(vmem_limit_bytes=32 * 2**20),
        cost_estimate=pl.CostEstimate(flops=2 * 128 * 256 * 3072, bytes_accessed=3 * 2**20, transcendentals=0),
        name="passage_scores",
    )(place.reshape(1), asked, passages, tails)

    merged = jnp.concatenate(
        [scores, jnp.tile(lse_parts.reshape(depth, own_rows), (plane, 1))], axis=1
    )
    back = lax.all_to_all(merged, BACK, 0, 0, tiled=True)

    ids = candidates.reshape(-1)
    shard, offset = ids // shard_rows, ids % shard_rows
    cores, ys = lax.axis_size("core"), lax.axis_size("y")
    row = (shard % cores) * (ys * depth) + (shard // cores % ys) * depth + shard // (cores * ys)
    own = lax.axis_index("core") * ys + lax.axis_index("y")
    lse_now, rerank = pl.pallas_call(
        lambda *refs: finish(full_width**-0.5, shard_rows, *refs),
        in_specs=[smem, smem, smem, vmem, smem],
        out_specs=[vmem, vmem],
        out_shape=[
            jax.ShapeDtypeStruct((1, own_rows), jnp.float32),
            jax.ShapeDtypeStruct((1, ids.shape[0]), jnp.float32),
        ],
        scratch_shapes=[pltpu.VMEM((128, 128), jnp.float32)],
        compiler_params=pltpu.CompilerParams(vmem_limit_bytes=32 * 2**20),
        name="finish",
    )(own.reshape(1), row, offset, back, lse_prev)
    return lse_now.reshape(-1), rerank


def solution(mesh):
    across, ways = mesh.devices.shape
    split = Mesh(mesh.devices.reshape(across // 8, 4, 2, ways), ALL)
    shard = ("z", "y", "core")
    return jax.shard_map(
        local,
        mesh=split,
        in_specs=(P(ALL, None), P(shard, None), P(ALL, None), P(ALL, None), P(ALL, None), P(ALL)),
        out_specs=(P(ALL), P(ALL, None)),
        check_vma=False,
    )
```

```python
import jax
import jax.numpy as jnp
from jax import lax
from jax.experimental import pallas as pl
from jax.experimental.pallas import tpu as pltpu
from jax.sharding import Mesh, PartitionSpec as P

ALL = ("z", "y", "core", "x")
PLANE = ("y", "core", "x")
BACK = ("core", "y", "z")
LOG2E = 1.4426950408889634
LANES = 128


def partial_lse(scale, rows, queries_ref, passages_ref, out_ref, scores):
    groups = queries_ref.shape[0]
    width = passages_ref.shape[1]
    block = queries_ref[:, :rows, :].reshape(groups * rows, width)
    count, step = passages_ref.shape[0], 256
    top = None
    for start in range(0, count, step):
        part = lax.dot_general(
            passages_ref[start : start + step, :],
            block,
            (((1,), (1,)), ((), ())),
            preferred_element_type=jnp.float32,
        )
        scores[start : start + step, :] = part
        high = jnp.max(part.reshape(step // 8, 8, groups * rows), axis=0)
        top = high if top is None else jnp.maximum(top, high)
    peak = jnp.max(top, axis=0, keepdims=True)
    total = None
    for start in range(0, count, step):
        part = jnp.exp2((scores[start : start + step, :] - peak) * (scale * LOG2E))
        added = jnp.sum(part.reshape(step // 8, 8, groups * rows), axis=0)
        total = added if total is None else total + added
    found = peak * scale + jnp.log(jnp.sum(total, axis=0, keepdims=True))
    first = pl.program_id(0) * groups

    @pl.when(first == 0)
    def _():
        out_ref[...] = jnp.zeros_like(out_ref)

    for group in range(groups):
        out_ref[pl.ds(first + group, 1), :rows] = found[:, group * rows : (group + 1) * rows]


def listed_scores(rows, place_ref, asked_ref, prefixes_ref, tails_ref, parts_ref, out_ref):
    shard_rows, head = tails_ref.shape[0], prefixes_ref.shape[1]
    full = head + tails_ref.shape[1]
    start = pl.multiple_of(place_ref[0] * shard_rows, shard_rows)
    dims = (((1,), (1,)), ((), ()))
    scores = lax.dot_general(
        asked_ref[:, :head], prefixes_ref[pl.ds(start, shard_rows), :], dims, preferred_element_type=jnp.float32
    ) + lax.dot_general(asked_ref[:, head:full], tails_ref[...], dims, preferred_element_type=jnp.float32)
    count = asked_ref.shape[0]
    shards = asked_ref[:, full : full + LANES].astype(jnp.float32)
    offsets = asked_ref[:, full + LANES : full + 2 * LANES].astype(jnp.float32)
    lanes = lax.broadcasted_iota(jnp.int32, (count, LANES), 1)
    mine = shards == place_ref[1].astype(jnp.float32)
    key = lanes.astype(jnp.float32) * shard_rows + offsets
    low = jnp.min(jnp.where(mine, key, float(LANES * shard_rows)), axis=1, keepdims=True)
    high = jnp.max(jnp.where(mine, key, 0.0), axis=1, keepdims=True)
    column = lax.broadcasted_iota(jnp.int32, scores.shape, 1)

    def pick(at):
        at = (at - jnp.floor(at * (1.0 / shard_rows)) * shard_rows).astype(jnp.int32)
        return jnp.sum(jnp.where(column == at, scores, 0.0), axis=1, keepdims=True)

    depth = parts_ref.shape[0]
    parts = jnp.concatenate([parts_ref[...]] * (count // depth), axis=0)
    out_ref[...] = jnp.where(lanes < rows, parts, jnp.where(lanes == rows, pick(low), pick(high)))


def finish(scale, rows, depth, own_ref, row_ref, second_ref, back_ref, prev_ref, lse_ref, rerank_ref):
    count = rerank_ref.shape[1]
    start = pl.multiple_of(own_ref[0] * depth, depth)
    parts = back_ref[pl.ds(start, depth), :rows]
    peak = jnp.max(parts, axis=0, keepdims=True)
    lse_ref[...] = peak + jnp.log(jnp.sum(jnp.exp(parts - peak), axis=0, keepdims=True))
    turned = back_ref[...].T
    shape = (8, LANES)
    at = jnp.broadcast_to(row_ref[...], shape)
    low = jnp.take_along_axis(jnp.broadcast_to(turned[rows : rows + 1, :], shape), at, axis=1)
    high = jnp.take_along_axis(jnp.broadcast_to(turned[rows + 1 : rows + 2, :], shape), at, axis=1)
    values = jnp.where(second_ref[...] > 0, high[:1], low[:1])
    rerank_ref[...] = values[:, :count] * scale - prev_ref[0]


def local(prefixes, tails, queries_now, queries_prev, candidates, lse_prev):
    vmem, smem = pl.BlockSpec(memory_space=pltpu.VMEM), pl.BlockSpec(memory_space=pltpu.SMEM)
    depth, ys, cores = lax.axis_size("z"), lax.axis_size("y"), lax.axis_size("core")
    own_rows, head = queries_now.shape
    shard_rows = tails.shape[0]
    full_width = queries_prev.shape[1]
    plane = ys * cores
    turn = depth // 2
    around = [(i + turn) % depth for i in range(depth)]

    ids = candidates.reshape(-1)
    count = ids.shape[0]
    shard, offset = ids // shard_rows, ids % shard_rows
    listed = jnp.concatenate(
        [jnp.pad(shard, (0, LANES - count), constant_values=-1), jnp.pad(offset, (0, LANES - count))]
    ).astype(queries_prev.dtype)

    passages = lax.all_to_all(
        jnp.broadcast_to(prefixes[None], (plane * lax.axis_size("x"),) + prefixes.shape),
        PLANE, 0, 0, tiled=True,
    ).reshape(-1, head)

    extra = full_width // head + 1
    sent = jnp.concatenate(
        [
            queries_now,
            queries_prev.reshape(extra - 1, head),
            listed.reshape(1, head),
            jnp.zeros((-extra % 16, head), queries_now.dtype),
        ]
    )
    column = lax.all_gather(sent, "z", axis_index_groups=[around])
    asked = column[:, own_rows : own_rows + extra].reshape(depth, extra * head)

    asked = jnp.broadcast_to(asked[None], (ys,) + asked.shape)
    asked, passages = lax.optimization_barrier((asked, passages))
    asked = lax.all_to_all(asked, "y", 0, 0, tiled=True).reshape(-1, extra * head)
    asked = lax.all_gather(asked, "core", tiled=True)

    step = 4
    parts = pl.pallas_call(
        lambda *refs: partial_lse(head**-0.5, own_rows, *refs),
        grid=(depth // step,),
        in_specs=[
            pl.BlockSpec((step,) + column.shape[1:], lambda i: (i, 0, 0)),
            pl.BlockSpec(passages.shape, lambda i: (0, 0)),
        ],
        out_specs=pl.BlockSpec((depth, LANES), lambda i: (0, 0)),
        out_shape=jax.ShapeDtypeStruct((depth, LANES), jnp.float32),
        scratch_shapes=[pltpu.VMEM((passages.shape[0], step * own_rows), jnp.float32)],
        compiler_params=pltpu.CompilerParams(vmem_limit_bytes=32 * 2**20),
        cost_estimate=pl.CostEstimate(flops=2 * 2**28, bytes_accessed=2 * 2**20, transcendentals=2**21),
        name="partial_lse",
    )(column, passages)

    z, y, core = lax.axis_index("z"), lax.axis_index("y"), lax.axis_index("core")
    place = y * cores + core
    merged = pl.pallas_call(
        lambda *refs: listed_scores(own_rows, *refs),
        in_specs=[smem, vmem, vmem, vmem, vmem],
        out_specs=vmem,
        out_shape=jax.ShapeDtypeStruct((plane * depth, LANES), jnp.float32),
        compiler_params=pltpu.CompilerParams(vmem_limit_bytes=32 * 2**20),
        cost_estimate=pl.CostEstimate(flops=2 * 128 * 256 * 3072, bytes_accessed=3 * 2**20, transcendentals=0),
        name="listed_scores",
    )(jnp.stack([place, z * plane + place]), asked, passages, tails, parts)

    groups = [base + i for base in range(0, plane * depth, depth) for i in around]
    back = lax.all_to_all(merged, BACK, 0, 0, tiled=True, axis_index_groups=[groups])

    row = (shard % cores) * (ys * depth) + (shard // cores % ys) * depth + (shard // plane + turn) % depth
    before = jnp.arange(count)[:, None] > jnp.arange(count)[None, :]
    second = jnp.any((shard[:, None] == shard[None, :]) & before, axis=1).astype(jnp.int32)
    lse_now, rerank = pl.pallas_call(
        lambda *refs: finish(full_width**-0.5, own_rows, depth, *refs),
        in_specs=[smem, vmem, vmem, vmem, smem],
        out_specs=[vmem, vmem],
        out_shape=[
            jax.ShapeDtypeStruct((1, own_rows), jnp.float32),
            jax.ShapeDtypeStruct((1, count), jnp.float32),
        ],
        compiler_params=pltpu.CompilerParams(vmem_limit_bytes=32 * 2**20),
        name="finish",
    )(
        (core * ys + y).reshape(1),
        jnp.pad(row, (0, LANES - count)).reshape(1, LANES),
        jnp.pad(second, (0, LANES - count)).reshape(1, LANES),
        back,
        lse_prev,
    )
    return lse_now.reshape(-1), rerank


def solution(mesh):
    across, ways = mesh.devices.shape
    split = Mesh(mesh.devices.reshape(across // 8, 4, 2, ways), ALL)
    shard = ("z", "y", "core")
    return jax.shard_map(
        local,
        mesh=split,
        in_specs=(P(ALL, None), P(shard, None), P(ALL, None), P(ALL, None), P(ALL, None), P(ALL)),
        out_specs=(P(ALL), P(ALL, None)),
        check_vma=False,
    )
```

```python
import jax
import jax.numpy as jnp
from jax import lax
from jax.experimental import pallas as pl
from jax.experimental.pallas import tpu as pltpu
from jax.sharding import Mesh, PartitionSpec as P

ALL = ("z", "y", "core", "x")
PLANE = ("core", "y", "x")
BACK = ("z", "y", "core")
PAIR = ("z", "core")
LOG2E = 1.4426950408889634
LANES = 128


def partial_lse(scale, rows, queries_ref, passages_ref, out_ref, scores):
    groups = queries_ref.shape[0]
    width = passages_ref.shape[1]
    block = queries_ref[:, :rows, :].reshape(groups * rows, width)
    count, step = passages_ref.shape[0], 256
    top = None
    for start in range(0, count, step):
        part = lax.dot_general(
            passages_ref[start : start + step, :],
            block,
            (((1,), (1,)), ((), ())),
            preferred_element_type=jnp.float32,
        )
        scores[start : start + step, :] = part
        high = jnp.max(part.reshape(step // 8, 8, groups * rows), axis=0)
        top = high if top is None else jnp.maximum(top, high)
    peak = jnp.max(top, axis=0, keepdims=True)
    total = None
    for start in range(0, count, step):
        part = jnp.exp2((scores[start : start + step, :] - peak) * (scale * LOG2E))
        added = jnp.sum(part.reshape(step // 8, 8, groups * rows), axis=0)
        total = added if total is None else total + added
    found = peak * scale + jnp.log(jnp.sum(total, axis=0, keepdims=True))
    first = pl.program_id(0) * groups

    @pl.when(first == 0)
    def _():
        out_ref[...] = jnp.zeros_like(out_ref)

    for group in range(groups):
        out_ref[pl.ds(first + group, 1), :rows] = found[:, group * rows : (group + 1) * rows]


def listed_scores(rows, place_ref, asked_ref, prefixes_ref, tails_ref, parts_ref, out_ref):
    shard_rows, head = tails_ref.shape[0], prefixes_ref.shape[1]
    full = head + tails_ref.shape[1]
    start = pl.multiple_of(place_ref[0] * shard_rows, shard_rows)
    dims = (((1,), (1,)), ((), ()))
    scores = lax.dot_general(
        asked_ref[:, :head], prefixes_ref[pl.ds(start, shard_rows), :], dims, preferred_element_type=jnp.float32
    ) + lax.dot_general(asked_ref[:, head:full], tails_ref[...], dims, preferred_element_type=jnp.float32)
    count = asked_ref.shape[0]
    shards = asked_ref[:, full : full + LANES].astype(jnp.float32)
    offsets = asked_ref[:, full + LANES : full + 2 * LANES].astype(jnp.float32)
    lanes = lax.broadcasted_iota(jnp.int32, (count, LANES), 1)
    mine = shards == place_ref[1].astype(jnp.float32)
    key = lanes.astype(jnp.float32) * shard_rows + offsets
    low = jnp.min(jnp.where(mine, key, float(LANES * shard_rows)), axis=1, keepdims=True)
    high = jnp.max(jnp.where(mine, key, 0.0), axis=1, keepdims=True)
    column = lax.broadcasted_iota(jnp.int32, scores.shape, 1)

    def pick(at):
        at = (at - jnp.floor(at * (1.0 / shard_rows)) * shard_rows).astype(jnp.int32)
        return jnp.sum(jnp.where(column == at, scores, 0.0), axis=1, keepdims=True)

    depth = parts_ref.shape[0]
    parts = jnp.concatenate([parts_ref[...]] * (count // depth), axis=0)
    out_ref[...] = jnp.where(lanes < rows, parts, jnp.where(lanes == rows, pick(low), pick(high)))


def finish(scale, rows, depth, own_ref, row_ref, second_ref, back_ref, prev_ref, lse_ref, rerank_ref):
    count = rerank_ref.shape[1]
    start = pl.multiple_of(own_ref[0] * depth, depth)
    parts = back_ref[pl.ds(start, depth), :rows]
    peak = jnp.max(parts, axis=0, keepdims=True)
    lse_ref[...] = peak + jnp.log(jnp.sum(jnp.exp(parts - peak), axis=0, keepdims=True))
    turned = back_ref[...].T
    shape = (8, LANES)
    at = jnp.broadcast_to(row_ref[...], shape)
    low = jnp.take_along_axis(jnp.broadcast_to(turned[rows : rows + 1, :], shape), at, axis=1)
    high = jnp.take_along_axis(jnp.broadcast_to(turned[rows + 1 : rows + 2, :], shape), at, axis=1)
    values = jnp.where(second_ref[...] > 0, high[:1], low[:1])
    rerank_ref[...] = values[:, :count] * scale - prev_ref[0]


def local(prefixes, tails, queries_now, queries_prev, candidates, lse_prev):
    vmem, smem = pl.BlockSpec(memory_space=pltpu.VMEM), pl.BlockSpec(memory_space=pltpu.SMEM)
    depth, ys, cores = lax.axis_size("z"), lax.axis_size("y"), lax.axis_size("core")
    own_rows, head = queries_now.shape
    shard_rows = tails.shape[0]
    full_width = queries_prev.shape[1]
    plane = ys * cores
    turn = depth // 2
    around = [(i + turn) % depth for i in range(depth)]

    ids = candidates.reshape(-1)
    count = ids.shape[0]
    shard, offset = ids // shard_rows, ids % shard_rows
    listed = jnp.concatenate(
        [jnp.pad(shard, (0, LANES - count), constant_values=-1), jnp.pad(offset, (0, LANES - count))]
    ).astype(queries_prev.dtype)

    passages = lax.all_to_all(
        jnp.broadcast_to(prefixes[None], (plane * lax.axis_size("x"),) + prefixes.shape),
        PLANE, 0, 0, tiled=True,
    ).reshape(-1, head)

    extra = full_width // head + 1
    sent = jnp.concatenate(
        [
            queries_now,
            queries_prev.reshape(extra - 1, head),
            listed.reshape(1, head),
            jnp.zeros((-extra % 16, head), queries_now.dtype),
        ]
    )
    rings = [[z * cores + (z + ring) % cores for z in around] for ring in range(cores)]
    column = lax.all_gather(sent, PAIR, axis_index_groups=rings)
    asked = column[:, own_rows : own_rows + extra].reshape(depth, extra * head)

    asked = jnp.broadcast_to(asked[None], (ys,) + asked.shape)
    asked, passages = lax.optimization_barrier((asked, passages))
    asked = lax.all_to_all(asked, "y", 0, 0, tiled=True).reshape(-1, extra * head)
    pairs = [[z * cores + (z + ring) % cores for ring in range(cores)] for z in range(depth)]
    asked = lax.all_gather(asked, PAIR, tiled=True, axis_index_groups=pairs)

    step = 4
    parts = pl.pallas_call(
        lambda *refs: partial_lse(head**-0.5, own_rows, *refs),
        grid=(depth // step,),
        in_specs=[
            pl.BlockSpec((step,) + column.shape[1:], lambda i: (i, 0, 0)),
            pl.BlockSpec(passages.shape, lambda i: (0, 0)),
        ],
        out_specs=pl.BlockSpec((depth, LANES), lambda i: (0, 0)),
        out_shape=jax.ShapeDtypeStruct((depth, LANES), jnp.float32),
        scratch_shapes=[pltpu.VMEM((passages.shape[0], step * own_rows), jnp.float32)],
        compiler_params=pltpu.CompilerParams(vmem_limit_bytes=32 * 2**20),
        cost_estimate=pl.CostEstimate(flops=2 * 2**28, bytes_accessed=2 * 2**20, transcendentals=2**21),
        name="partial_lse",
    )(column, passages)

    z, y, core = lax.axis_index("z"), lax.axis_index("y"), lax.axis_index("core")
    place = y * cores + core
    merged = pl.pallas_call(
        lambda *refs: listed_scores(own_rows, *refs),
        in_specs=[smem, vmem, vmem, vmem, vmem],
        out_specs=vmem,
        out_shape=jax.ShapeDtypeStruct((plane * depth, LANES), jnp.float32),
        compiler_params=pltpu.CompilerParams(vmem_limit_bytes=32 * 2**20),
        cost_estimate=pl.CostEstimate(flops=2 * 128 * 256 * 3072, bytes_accessed=3 * 2**20, transcendentals=0),
        name="listed_scores",
    )(jnp.stack([core * ys + y, z * plane + place]), asked, passages, tails, parts)

    groups = [z * plane + i * cores + (z + ring) % cores for ring in range(cores) for i in range(ys) for z in around]
    back = lax.all_to_all(merged, BACK, 0, 0, tiled=True, axis_index_groups=[groups])

    far = shard // plane
    row = ((shard + far) % cores * ys + shard // cores % ys) * depth + (far + turn) % depth
    before = jnp.arange(count)[:, None] > jnp.arange(count)[None, :]
    second = jnp.any((shard[:, None] == shard[None, :]) & before, axis=1).astype(jnp.int32)
    lse_now, rerank = pl.pallas_call(
        lambda *refs: finish(full_width**-0.5, own_rows, depth, *refs),
        in_specs=[smem, vmem, vmem, vmem, smem],
        out_specs=[vmem, vmem],
        out_shape=[
            jax.ShapeDtypeStruct((1, own_rows), jnp.float32),
            jax.ShapeDtypeStruct((1, count), jnp.float32),
        ],
        compiler_params=pltpu.CompilerParams(vmem_limit_bytes=32 * 2**20),
        name="finish",
    )(
        ((core + z) % cores * ys + y).reshape(1),
        jnp.pad(row, (0, LANES - count)).reshape(1, LANES),
        jnp.pad(second, (0, LANES - count)).reshape(1, LANES),
        back,
        lse_prev,
    )
    return lse_now.reshape(-1), rerank


def solution(mesh):
    across, ways = mesh.devices.shape
    split = Mesh(mesh.devices.reshape(across // 8, 4, 2, ways), ALL)
    shard = ("z", "y", "core")
    return jax.shard_map(
        local,
        mesh=split,
        in_specs=(P(ALL, None), P(shard, None), P(ALL, None), P(ALL, None), P(ALL, None), P(ALL)),
        out_specs=(P(ALL), P(ALL, None)),
        check_vma=False,
    )
```

```python
import jax
import jax.numpy as jnp
from jax import lax
from jax.experimental import pallas as pl
from jax.experimental.pallas import tpu as pltpu
from jax.sharding import Mesh, PartitionSpec as P

ALL = ("z", "y", "core", "x")
PLANE = ("core", "y", "x")
BACK = ("z", "y", "core")
PAIR = ("z", "core")
LOG2E = 1.4426950408889634
LANES = 128


def partial_lse(scale, rows, queries_ref, passages_ref, out_ref, scores):
    groups = queries_ref.shape[0]
    width = passages_ref.shape[1]
    block = queries_ref[:, :rows, :].reshape(groups * rows, width)
    count, step = passages_ref.shape[0], 256
    top = None
    for start in range(0, count, step):
        part = lax.dot_general(
            passages_ref[start : start + step, :],
            block,
            (((1,), (1,)), ((), ())),
            preferred_element_type=jnp.float32,
        )
        scores[start : start + step, :] = part
        high = jnp.max(part.reshape(step // 8, 8, groups * rows), axis=0)
        top = high if top is None else jnp.maximum(top, high)
    peak = jnp.max(top, axis=0, keepdims=True)
    total = None
    for start in range(0, count, step):
        part = jnp.exp2((scores[start : start + step, :] - peak) * (scale * LOG2E))
        added = jnp.sum(part.reshape(step // 8, 8, groups * rows), axis=0)
        total = added if total is None else total + added
    found = peak * scale + jnp.log(jnp.sum(total, axis=0, keepdims=True))
    first = pl.program_id(0) * groups

    @pl.when(first == 0)
    def _():
        out_ref[...] = jnp.zeros_like(out_ref)

    for group in range(groups):
        out_ref[pl.ds(first + group, 1), :rows] = found[:, group * rows : (group + 1) * rows]


def listed_scores(rows, place_ref, asked_ref, prefixes_ref, tails_ref, parts_ref, out_ref):
    shard_rows, head = tails_ref.shape[0], prefixes_ref.shape[1]
    full = head + tails_ref.shape[1]
    start = pl.multiple_of(place_ref[0] * shard_rows, shard_rows)
    dims = (((1,), (1,)), ((), ()))
    scores = lax.dot_general(
        asked_ref[:, :head], prefixes_ref[pl.ds(start, shard_rows), :], dims, preferred_element_type=jnp.float32
    ) + lax.dot_general(asked_ref[:, head:full], tails_ref[...], dims, preferred_element_type=jnp.float32)
    count = asked_ref.shape[0]
    shards = asked_ref[:, full : full + LANES].astype(jnp.float32)
    offsets = asked_ref[:, full + LANES : full + 2 * LANES].astype(jnp.float32)
    lanes = lax.broadcasted_iota(jnp.int32, (count, LANES), 1)
    mine = shards == place_ref[1].astype(jnp.float32)
    key = lanes.astype(jnp.float32) * shard_rows + offsets
    low = jnp.min(jnp.where(mine, key, float(LANES * shard_rows)), axis=1, keepdims=True)
    high = jnp.max(jnp.where(mine, key, 0.0), axis=1, keepdims=True)
    column = lax.broadcasted_iota(jnp.int32, scores.shape, 1)

    def pick(at):
        at = (at - jnp.floor(at * (1.0 / shard_rows)) * shard_rows).astype(jnp.int32)
        return jnp.sum(jnp.where(column == at, scores, 0.0), axis=1, keepdims=True)

    depth = parts_ref.shape[0]
    parts = jnp.concatenate([parts_ref[...]] * (count // depth), axis=0)
    out_ref[...] = jnp.where(lanes < rows, parts, jnp.where(lanes == rows, pick(low), pick(high)))


def finish(scale, rows, depth, own_ref, row_ref, second_ref, back_ref, prev_ref, lse_ref, rerank_ref):
    count = rerank_ref.shape[1]
    start = pl.multiple_of(own_ref[0] * depth, depth)
    parts = back_ref[pl.ds(start, depth), :rows]
    peak = jnp.max(parts, axis=0, keepdims=True)
    lse_ref[...] = peak + jnp.log(jnp.sum(jnp.exp(parts - peak), axis=0, keepdims=True))
    turned = back_ref[...].T
    shape = (8, LANES)
    at = jnp.broadcast_to(row_ref[...], shape)
    low = jnp.take_along_axis(jnp.broadcast_to(turned[rows : rows + 1, :], shape), at, axis=1)
    high = jnp.take_along_axis(jnp.broadcast_to(turned[rows + 1 : rows + 2, :], shape), at, axis=1)
    values = jnp.where(second_ref[...] > 0, high[:1], low[:1])
    rerank_ref[...] = values[:, :count] * scale - prev_ref[0]


def local(prefixes, tails, queries_now, queries_prev, candidates, lse_prev):
    vmem, smem = pl.BlockSpec(memory_space=pltpu.VMEM), pl.BlockSpec(memory_space=pltpu.SMEM)
    depth, ys, cores = lax.axis_size("z"), lax.axis_size("y"), lax.axis_size("core")
    own_rows, head = queries_now.shape
    shard_rows = tails.shape[0]
    full_width = queries_prev.shape[1]
    plane = ys * cores
    turn = depth // 2
    around = [(i + turn) % depth for i in range(depth)]

    ids = candidates.reshape(-1)
    count = ids.shape[0]
    shard, offset = ids // shard_rows, ids % shard_rows
    listed = jnp.concatenate(
        [jnp.pad(shard, (0, LANES - count), constant_values=-1), jnp.pad(offset, (0, LANES - count))]
    ).astype(queries_prev.dtype)

    passages = lax.all_to_all(
        jnp.broadcast_to(prefixes[None], (plane * lax.axis_size("x"),) + prefixes.shape),
        PLANE, 0, 0, tiled=True,
    ).reshape(-1, head)

    extra = full_width // head + 1
    sent = jnp.concatenate(
        [
            queries_now,
            queries_prev.reshape(extra - 1, head),
            listed.reshape(1, head),
            jnp.zeros((-extra % 16, head), queries_now.dtype),
        ]
    )
    orders = [around, around[::-1]]
    rings = [[z * cores + (z + ring) % cores for z in orders[ring]] for ring in range(cores)]
    column = lax.all_gather(sent, PAIR, axis_index_groups=rings)
    asked = column[:, own_rows : own_rows + extra].reshape(depth, extra * head)

    asked = jnp.broadcast_to(asked[None], (ys,) + asked.shape)
    asked, passages = lax.optimization_barrier((asked, passages))
    asked = lax.all_to_all(asked, "y", 0, 0, tiled=True).reshape(-1, extra * head)
    pairs = [[z * cores + (z + ring) % cores for ring in range(cores)] for z in range(depth)]
    asked = lax.all_gather(asked, PAIR, tiled=True, axis_index_groups=pairs)

    step = 4
    parts = pl.pallas_call(
        lambda *refs: partial_lse(head**-0.5, own_rows, *refs),
        grid=(depth // step,),
        in_specs=[
            pl.BlockSpec((step,) + column.shape[1:], lambda i: (i, 0, 0)),
            pl.BlockSpec(passages.shape, lambda i: (0, 0)),
        ],
        out_specs=pl.BlockSpec((depth, LANES), lambda i: (0, 0)),
        out_shape=jax.ShapeDtypeStruct((depth, LANES), jnp.float32),
        scratch_shapes=[pltpu.VMEM((passages.shape[0], step * own_rows), jnp.float32)],
        compiler_params=pltpu.CompilerParams(vmem_limit_bytes=32 * 2**20),
        cost_estimate=pl.CostEstimate(flops=2 * 2**28, bytes_accessed=2 * 2**20, transcendentals=2**21),
        name="partial_lse",
    )(column, passages)

    z, y, core = lax.axis_index("z"), lax.axis_index("y"), lax.axis_index("core")
    place = y * cores + core
    merged = pl.pallas_call(
        lambda *refs: listed_scores(own_rows, *refs),
        in_specs=[smem, vmem, vmem, vmem, vmem],
        out_specs=vmem,
        out_shape=jax.ShapeDtypeStruct((plane * depth, LANES), jnp.float32),
        compiler_params=pltpu.CompilerParams(vmem_limit_bytes=32 * 2**20),
        cost_estimate=pl.CostEstimate(flops=2 * 128 * 256 * 3072, bytes_accessed=3 * 2**20, transcendentals=0),
        name="listed_scores",
    )(jnp.stack([core * ys + y, z * plane + place]), asked, passages, tails, parts)

    groups = [z * plane + i * cores + (z + ring) % cores for ring in range(cores) for i in range(ys) for z in orders[ring]]
    back = lax.all_to_all(merged, BACK, 0, 0, tiled=True, axis_index_groups=[groups])

    far = shard // plane
    ring, at = (shard + far) % cores, (far + turn) % depth
    row = (ring * ys + shard // cores % ys) * depth + jnp.where(ring == 0, at, depth - 1 - at)
    before = jnp.arange(count)[:, None] > jnp.arange(count)[None, :]
    second = jnp.any((shard[:, None] == shard[None, :]) & before, axis=1).astype(jnp.int32)
    lse_now, rerank = pl.pallas_call(
        lambda *refs: finish(full_width**-0.5, own_rows, depth, *refs),
        in_specs=[smem, vmem, vmem, vmem, smem],
        out_specs=[vmem, vmem],
        out_shape=[
            jax.ShapeDtypeStruct((1, own_rows), jnp.float32),
            jax.ShapeDtypeStruct((1, count), jnp.float32),
        ],
        compiler_params=pltpu.CompilerParams(vmem_limit_bytes=32 * 2**20),
        name="finish",
    )(
        ((core + z) % cores * ys + y).reshape(1),
        jnp.pad(row, (0, LANES - count)).reshape(1, LANES),
        jnp.pad(second, (0, LANES - count)).reshape(1, LANES),
        back,
        lse_prev,
    )
    return lse_now.reshape(-1), rerank


def solution(mesh):
    across, ways = mesh.devices.shape
    split = Mesh(mesh.devices.reshape(across // 8, 4, 2, ways), ALL)
    shard = ("z", "y", "core")
    return jax.shard_map(
        local,
        mesh=split,
        in_specs=(P(ALL, None), P(shard, None), P(ALL, None), P(ALL, None), P(ALL, None), P(ALL)),
        out_specs=(P(ALL), P(ALL, None)),
        check_vma=False,
    )
```

```python
import jax
import jax.numpy as jnp
from jax import lax
from jax.experimental import pallas as pl
from jax.experimental.pallas import tpu as pltpu
from jax.sharding import Mesh, PartitionSpec as P

ALL = ("z", "y", "core", "x")
PLANE = ("core", "y", "x")
BACK = ("z", "y", "core")
PAIR = ("z", "core")
LOG2E = 1.4426950408889634
LANES = 128


def partial_lse(scale, rows, queries_ref, passages_ref, out_ref, scores):
    groups = queries_ref.shape[0]
    width = passages_ref.shape[1]
    block = queries_ref[:, :rows, :].reshape(groups * rows, width)
    count, step = passages_ref.shape[0], 256
    top = None
    for start in range(0, count, step):
        part = lax.dot_general(
            passages_ref[start : start + step, :],
            block,
            (((1,), (1,)), ((), ())),
            preferred_element_type=jnp.float32,
        )
        scores[start : start + step, :] = part
        high = jnp.max(part.reshape(step // 8, 8, groups * rows), axis=0)
        top = high if top is None else jnp.maximum(top, high)
    peak = jnp.max(top, axis=0, keepdims=True)
    total = None
    for start in range(0, count, step):
        part = jnp.exp2((scores[start : start + step, :] - peak) * (scale * LOG2E))
        added = jnp.sum(part.reshape(step // 8, 8, groups * rows), axis=0)
        total = added if total is None else total + added
    found = peak * scale + jnp.log(jnp.sum(total, axis=0, keepdims=True))
    first = pl.program_id(0) * groups

    @pl.when(first == 0)
    def _():
        out_ref[...] = jnp.zeros_like(out_ref)

    for group in range(groups):
        out_ref[pl.ds(first + group, 1), :rows] = found[:, group * rows : (group + 1) * rows]


def listed_scores(rows, asked_ref, prefixes_ref, tails_ref, parts_ref, out_ref):
    shard_rows, head = tails_ref.shape[0], prefixes_ref.shape[1]
    full = head + tails_ref.shape[1]
    z, y, core = lax.axis_index("z"), lax.axis_index("y"), lax.axis_index("core")
    ys, cores = lax.axis_size("y"), lax.axis_size("core")
    start = pl.multiple_of((core * ys + y) * shard_rows, shard_rows)
    dims = (((1,), (1,)), ((), ()))
    scores = lax.dot_general(
        asked_ref[:, :head], prefixes_ref[pl.ds(start, shard_rows), :], dims, preferred_element_type=jnp.float32
    ) + lax.dot_general(asked_ref[:, head:full], tails_ref[...], dims, preferred_element_type=jnp.float32)
    count = asked_ref.shape[0]
    shards = asked_ref[:, full : full + LANES].astype(jnp.float32)
    offsets = asked_ref[:, full + LANES : full + 2 * LANES].astype(jnp.float32)
    lanes = lax.broadcasted_iota(jnp.int32, (count, LANES), 1)
    mine = shards == ((z * ys + y) * cores + core).astype(jnp.float32)
    key = lanes.astype(jnp.float32) * shard_rows + offsets
    low = jnp.min(jnp.where(mine, key, float(LANES * shard_rows)), axis=1, keepdims=True)
    high = jnp.max(jnp.where(mine, key, 0.0), axis=1, keepdims=True)
    column = lax.broadcasted_iota(jnp.int32, scores.shape, 1)

    def pick(at):
        at = (at - jnp.floor(at * (1.0 / shard_rows)) * shard_rows).astype(jnp.int32)
        return jnp.sum(jnp.where(column == at, scores, 0.0), axis=1, keepdims=True)

    depth = parts_ref.shape[0]
    parts = jnp.concatenate([parts_ref[...]] * (count // depth), axis=0)
    out_ref[...] = jnp.where(lanes < rows, parts, jnp.where(lanes == rows, pick(low), pick(high)))


def finish(scale, rows, depth, row_ref, second_ref, back_ref, prev_ref, lse_ref, rerank_ref):
    count = rerank_ref.shape[1]
    cores = lax.axis_size("core")
    ring = (lax.axis_index("z") + lax.axis_index("core")) % cores
    start = pl.multiple_of((ring * lax.axis_size("y") + lax.axis_index("y")) * depth, depth)
    parts = back_ref[pl.ds(start, depth), :rows]
    peak = jnp.max(parts, axis=0, keepdims=True)
    lse_ref[...] = peak + jnp.log(jnp.sum(jnp.exp(parts - peak), axis=0, keepdims=True))
    turned = back_ref[...].T
    shape = (8, LANES)
    at = jnp.broadcast_to(row_ref[...], shape)
    low = jnp.take_along_axis(jnp.broadcast_to(turned[rows : rows + 1, :], shape), at, axis=1)
    high = jnp.take_along_axis(jnp.broadcast_to(turned[rows + 1 : rows + 2, :], shape), at, axis=1)
    values = jnp.where(second_ref[...] > 0, high[:1], low[:1])
    rerank_ref[...] = values[:, :count] * scale - prev_ref[0]


def local(prefixes, tails, queries_now, queries_prev, candidates, lse_prev):
    vmem, smem = pl.BlockSpec(memory_space=pltpu.VMEM), pl.BlockSpec(memory_space=pltpu.SMEM)
    depth, ys, cores = lax.axis_size("z"), lax.axis_size("y"), lax.axis_size("core")
    own_rows, head = queries_now.shape
    shard_rows = tails.shape[0]
    full_width = queries_prev.shape[1]
    plane = ys * cores
    turn = depth // 2
    around = [(i + turn) % depth for i in range(depth)]

    ids = candidates.reshape(-1)
    count = ids.shape[0]
    shard, offset = ids // shard_rows, ids % shard_rows
    listed = jnp.concatenate(
        [jnp.pad(shard, (0, LANES - count), constant_values=-1), jnp.pad(offset, (0, LANES - count))]
    ).astype(queries_prev.dtype)

    passages = lax.all_to_all(
        jnp.broadcast_to(prefixes[None], (plane * lax.axis_size("x"),) + prefixes.shape),
        PLANE, 0, 0, tiled=True,
    ).reshape(-1, head)

    extra = full_width // head + 1
    sent = jnp.concatenate(
        [
            queries_now,
            queries_prev.reshape(extra - 1, head),
            listed.reshape(1, head),
            jnp.zeros((-extra % 16, head), queries_now.dtype),
        ]
    )
    orders = [around, around[::-1]]
    rings = [[z * cores + (z + ring) % cores for z in orders[ring]] for ring in range(cores)]
    column = lax.all_gather(sent, PAIR, axis_index_groups=rings)
    asked = column[:, own_rows : own_rows + extra].reshape(depth, extra * head)

    asked = jnp.broadcast_to(asked[None], (ys,) + asked.shape)
    asked, passages = lax.optimization_barrier((asked, passages))
    asked = lax.all_to_all(asked, "y", 0, 0, tiled=True).reshape(-1, extra * head)
    pairs = [[z * cores + (z + ring) % cores for ring in range(cores)] for z in range(depth)]
    asked = lax.all_gather(asked, PAIR, tiled=True, axis_index_groups=pairs)

    step = 4
    parts = pl.pallas_call(
        lambda *refs: partial_lse(head**-0.5, own_rows, *refs),
        grid=(depth // step,),
        in_specs=[
            pl.BlockSpec((step,) + column.shape[1:], lambda i: (i, 0, 0)),
            pl.BlockSpec(passages.shape, lambda i: (0, 0)),
        ],
        out_specs=pl.BlockSpec((depth, LANES), lambda i: (0, 0)),
        out_shape=jax.ShapeDtypeStruct((depth, LANES), jnp.float32),
        scratch_shapes=[pltpu.VMEM((passages.shape[0], step * own_rows), jnp.float32)],
        compiler_params=pltpu.CompilerParams(vmem_limit_bytes=32 * 2**20),
        cost_estimate=pl.CostEstimate(flops=2 * 2**28, bytes_accessed=2 * 2**20, transcendentals=2**21),
        name="partial_lse",
    )(column, passages)

    z, y, core = lax.axis_index("z"), lax.axis_index("y"), lax.axis_index("core")
    merged = pl.pallas_call(
        lambda *refs: listed_scores(own_rows, *refs),
        in_specs=[vmem, vmem, vmem, vmem],
        out_specs=vmem,
        out_shape=jax.ShapeDtypeStruct((plane * depth, LANES), jnp.float32),
        compiler_params=pltpu.CompilerParams(vmem_limit_bytes=32 * 2**20),
        cost_estimate=pl.CostEstimate(flops=2 * 128 * 256 * 3072, bytes_accessed=3 * 2**20, transcendentals=0),
        name="listed_scores",
    )(asked, passages, tails, parts)

    groups = [z * plane + i * cores + (z + ring) % cores for ring in range(cores) for i in range(ys) for z in orders[ring]]
    back = lax.all_to_all(merged, BACK, 0, 0, tiled=True, axis_index_groups=[groups])

    far = shard // plane
    ring, at = (shard + far) % cores, (far + turn) % depth
    row = (ring * ys + shard // cores % ys) * depth + jnp.where(ring == 0, at, depth - 1 - at)
    before = jnp.arange(count)[:, None] > jnp.arange(count)[None, :]
    second = jnp.any((shard[:, None] == shard[None, :]) & before, axis=1).astype(jnp.int32)
    lse_now, rerank = pl.pallas_call(
        lambda *refs: finish(full_width**-0.5, own_rows, depth, *refs),
        in_specs=[vmem, vmem, vmem, smem],
        out_specs=[vmem, vmem],
        out_shape=[
            jax.ShapeDtypeStruct((1, own_rows), jnp.float32),
            jax.ShapeDtypeStruct((1, count), jnp.float32),
        ],
        compiler_params=pltpu.CompilerParams(vmem_limit_bytes=32 * 2**20),
        name="finish",
    )(
        jnp.pad(row, (0, LANES - count)).reshape(1, LANES),
        jnp.pad(second, (0, LANES - count)).reshape(1, LANES),
        back,
        lse_prev,
    )
    return lse_now.reshape(-1), rerank


def solution(mesh):
    across, ways = mesh.devices.shape
    split = Mesh(mesh.devices.reshape(across // 8, 4, 2, ways), ALL)
    shard = ("z", "y", "core")
    return jax.shard_map(
        local,
        mesh=split,
        in_specs=(P(ALL, None), P(shard, None), P(ALL, None), P(ALL, None), P(ALL, None), P(ALL)),
        out_specs=(P(ALL), P(ALL, None)),
        check_vma=False,
    )
```

```python
import jax
import jax.numpy as jnp
from jax import lax
from jax.experimental import pallas as pl
from jax.experimental.pallas import tpu as pltpu
from jax.sharding import Mesh, PartitionSpec as P

ALL = ("z", "y", "core", "x")
PLANE = ("core", "y", "x")
BACK = ("z", "y", "core")
PAIR = ("z", "core")
LOG2E = 1.4426950408889634
LANES = 128


def partial_lse(scale, rows, queries_ref, passages_ref, out_ref, scores):
    groups = queries_ref.shape[0]
    width = passages_ref.shape[1]
    block = queries_ref[:, :rows, :].reshape(groups * rows, width)
    count, step = passages_ref.shape[0], 256
    top = None
    for start in range(0, count, step):
        part = lax.dot_general(
            passages_ref[start : start + step, :],
            block,
            (((1,), (1,)), ((), ())),
            preferred_element_type=jnp.float32,
        )
        scores[start : start + step, :] = part
        high = jnp.max(part.reshape(step // 8, 8, groups * rows), axis=0)
        top = high if top is None else jnp.maximum(top, high)
    peak = jnp.max(top, axis=0, keepdims=True)
    total = None
    for start in range(0, count, step):
        part = jnp.exp2((scores[start : start + step, :] - peak) * (scale * LOG2E))
        added = jnp.sum(part.reshape(step // 8, 8, groups * rows), axis=0)
        total = added if total is None else total + added
    found = peak * scale + jnp.log(jnp.sum(total, axis=0, keepdims=True))
    first = pl.program_id(0) * groups

    @pl.when(first == 0)
    def _():
        out_ref[...] = jnp.zeros_like(out_ref)

    for group in range(groups):
        out_ref[pl.ds(first + group, 1), LANES - rows :] = found[:, group * rows : (group + 1) * rows]


def listed_scores(rows, asked_ref, prefixes_ref, tails_ref, parts_ref, out_ref):
    shard_rows, head = tails_ref.shape[0], prefixes_ref.shape[1]
    full = head + tails_ref.shape[1]
    z, y, core = lax.axis_index("z"), lax.axis_index("y"), lax.axis_index("core")
    ys, cores = lax.axis_size("y"), lax.axis_size("core")
    start = pl.multiple_of((core * ys + y) * shard_rows, shard_rows)
    dims = (((1,), (1,)), ((), ()))
    scores = lax.dot_general(
        prefixes_ref[pl.ds(start, shard_rows), :], asked_ref[:, :head], dims, preferred_element_type=jnp.float32
    ) + lax.dot_general(tails_ref[...], asked_ref[:, head:full], dims, preferred_element_type=jnp.float32)
    count, depth = asked_ref.shape[0], parts_ref.shape[0]
    shards = asked_ref[:, full : full + LANES].astype(jnp.float32).T
    offsets = asked_ref[:, full + LANES : full + 2 * LANES].astype(jnp.float32).T
    mine = shards == ((z * ys + y) * cores + core).astype(jnp.float32)
    key = lax.broadcasted_iota(jnp.int32, shards.shape, 0).astype(jnp.float32) * shard_rows + offsets
    low = jnp.min(jnp.where(mine, key, float(LANES * shard_rows)), axis=0, keepdims=True)
    high = jnp.max(jnp.where(mine, key, 0.0), axis=0, keepdims=True)
    row = lax.broadcasted_iota(jnp.int32, scores.shape, 0)

    def pick(at):
        at = (at - jnp.floor(at * (1.0 / shard_rows)) * shard_rows).astype(jnp.int32)
        return jnp.sum(jnp.where(row == at, scores, 0.0), axis=0, keepdims=True)

    slots = lax.broadcasted_iota(jnp.int32, (8, count), 0)
    values = jnp.where(slots == 0, pick(low), jnp.where(slots == 1, pick(high), 0.0))
    values = jnp.concatenate([values, jnp.zeros((LANES - 8, count), jnp.float32)], axis=0).T
    lanes = lax.broadcasted_iota(jnp.int32, (count, LANES), 1)
    out_ref[...] = jnp.where(lanes < 8, values, jnp.concatenate([parts_ref[...]] * (count // depth), axis=0))


def finish(scale, rows, depth, row_ref, second_ref, back_ref, prev_ref, lse_ref, rerank_ref):
    count = rerank_ref.shape[1]
    cores = lax.axis_size("core")
    ring = (lax.axis_index("z") + lax.axis_index("core")) % cores
    start = pl.multiple_of((ring * lax.axis_size("y") + lax.axis_index("y")) * depth, depth)
    parts = back_ref[pl.ds(start, depth), LANES - rows :]
    peak = jnp.max(parts, axis=0, keepdims=True)
    lse_ref[...] = peak + jnp.log(jnp.sum(jnp.exp(parts - peak), axis=0, keepdims=True))
    turned = back_ref[...].T
    shape = (8, LANES)
    at = jnp.broadcast_to(row_ref[...], shape)
    low = jnp.take_along_axis(jnp.broadcast_to(turned[:1, :], shape), at, axis=1)
    high = jnp.take_along_axis(jnp.broadcast_to(turned[1:2, :], shape), at, axis=1)
    values = jnp.where(second_ref[...] > 0, high[:1], low[:1])
    rerank_ref[...] = values[:, :count] * scale - prev_ref[...]


def local(prefixes, tails, queries_now, queries_prev, candidates, lse_prev):
    vmem, smem = pl.BlockSpec(memory_space=pltpu.VMEM), pl.BlockSpec(memory_space=pltpu.SMEM)
    depth, ys, cores = lax.axis_size("z"), lax.axis_size("y"), lax.axis_size("core")
    own_rows, head = queries_now.shape
    shard_rows = tails.shape[0]
    full_width = queries_prev.shape[1]
    plane = ys * cores
    turn = depth // 2
    around = [(i + turn) % depth for i in range(depth)]

    ids = candidates.reshape(-1)
    count = ids.shape[0]
    shard, offset = ids // shard_rows, ids % shard_rows
    listed = jnp.concatenate(
        [jnp.pad(shard, (0, LANES - count), constant_values=-1), jnp.pad(offset, (0, LANES - count))]
    ).astype(queries_prev.dtype)

    passages = lax.all_to_all(
        jnp.broadcast_to(prefixes[None], (plane * lax.axis_size("x"),) + prefixes.shape),
        PLANE, 0, 0, tiled=True,
    ).reshape(-1, head)

    extra = full_width // head + 1
    sent = jnp.concatenate(
        [
            queries_now,
            queries_prev.reshape(extra - 1, head),
            listed.reshape(1, head),
            jnp.zeros((-extra % 16, head), queries_now.dtype),
        ]
    )
    orders = [around, around[::-1]]
    rings = [[z * cores + (z + ring) % cores for z in orders[ring]] for ring in range(cores)]
    column = lax.all_gather(sent, PAIR, axis_index_groups=rings)
    asked = column[:, own_rows : own_rows + extra].reshape(depth, extra * head)

    asked = jnp.broadcast_to(asked[None], (ys,) + asked.shape)
    asked, passages = lax.optimization_barrier((asked, passages))
    asked = lax.all_to_all(asked, "y", 0, 0, tiled=True).reshape(-1, extra * head)
    pairs = [[z * cores + (z + ring) % cores for ring in range(cores)] for z in range(depth)]
    asked = lax.all_gather(asked, PAIR, tiled=True, axis_index_groups=pairs)

    step = 4
    parts = pl.pallas_call(
        lambda *refs: partial_lse(head**-0.5, own_rows, *refs),
        grid=(depth // step,),
        in_specs=[
            pl.BlockSpec((step,) + column.shape[1:], lambda i: (i, 0, 0)),
            pl.BlockSpec(passages.shape, lambda i: (0, 0)),
        ],
        out_specs=pl.BlockSpec((depth, LANES), lambda i: (0, 0)),
        out_shape=jax.ShapeDtypeStruct((depth, LANES), jnp.float32),
        scratch_shapes=[pltpu.VMEM((passages.shape[0], step * own_rows), jnp.float32)],
        compiler_params=pltpu.CompilerParams(vmem_limit_bytes=32 * 2**20),
        cost_estimate=pl.CostEstimate(flops=2 * 2**28, bytes_accessed=2 * 2**20, transcendentals=2**21),
        name="partial_lse",
    )(column, passages)

    z, y, core = lax.axis_index("z"), lax.axis_index("y"), lax.axis_index("core")
    merged = pl.pallas_call(
        lambda *refs: listed_scores(own_rows, *refs),
        in_specs=[vmem, vmem, vmem, vmem],
        out_specs=vmem,
        out_shape=jax.ShapeDtypeStruct((plane * depth, LANES), jnp.float32),
        compiler_params=pltpu.CompilerParams(vmem_limit_bytes=32 * 2**20),
        cost_estimate=pl.CostEstimate(flops=2 * 128 * 256 * 3072, bytes_accessed=3 * 2**20, transcendentals=0),
        name="listed_scores",
    )(asked, passages, tails, parts)

    groups = [z * plane + i * cores + (z + ring) % cores for ring in range(cores) for i in range(ys) for z in orders[ring]]
    back = lax.all_to_all(merged, BACK, 0, 0, tiled=True, axis_index_groups=[groups])

    far = shard // plane
    ring, at = (shard + far) % cores, (far + turn) % depth
    row = (ring * ys + shard // cores % ys) * depth + jnp.where(ring == 0, at, depth - 1 - at)
    before = jnp.arange(count)[:, None] > jnp.arange(count)[None, :]
    second = jnp.any((shard[:, None] == shard[None, :]) & before, axis=1).astype(jnp.int32)
    lse_now, rerank = pl.pallas_call(
        lambda *refs: finish(full_width**-0.5, own_rows, depth, *refs),
        in_specs=[vmem, vmem, vmem, vmem],
        out_specs=[vmem, vmem],
        out_shape=[
            jax.ShapeDtypeStruct((1, own_rows), jnp.float32),
            jax.ShapeDtypeStruct((1, count), jnp.float32),
        ],
        compiler_params=pltpu.CompilerParams(vmem_limit_bytes=32 * 2**20),
        name="finish",
    )(
        jnp.pad(row, (0, LANES - count)).reshape(1, LANES),
        jnp.pad(second, (0, LANES - count)).reshape(1, LANES),
        back,
        lse_prev.reshape(1, 1),
    )
    return lse_now.reshape(-1), rerank


def solution(mesh):
    across, ways = mesh.devices.shape
    split = Mesh(mesh.devices.reshape(across // 8, 4, 2, ways), ALL)
    shard = ("z", "y", "core")
    return jax.shard_map(
        local,
        mesh=split,
        in_specs=(P(ALL, None), P(shard, None), P(ALL, None), P(ALL, None), P(ALL, None), P(ALL)),
        out_specs=(P(ALL), P(ALL, None)),
        check_vma=False,
    )
```

```python
import jax
import jax.numpy as jnp
from jax import lax
from jax.experimental import pallas as pl
from jax.experimental.pallas import tpu as pltpu
from jax.sharding import Mesh, PartitionSpec as P

ALL = ("z", "y", "core", "x")
PLANE = ("core", "y", "x")
BACK = ("z", "y", "core")
PAIR = ("z", "core")
LOG2E = 1.4426950408889634
LANES = 128


def partial_lse(scale, rows, queries_ref, passages_ref, out_ref, scores):
    groups = queries_ref.shape[0]
    width = passages_ref.shape[1]
    block = queries_ref[:, :rows, :].reshape(groups * rows, width)
    count, step = passages_ref.shape[0], 256
    top = None
    for start in range(0, count, step):
        part = lax.dot_general(
            passages_ref[start : start + step, :],
            block,
            (((1,), (1,)), ((), ())),
            preferred_element_type=jnp.float32,
        )
        scores[start : start + step, :] = part
        high = jnp.max(part.reshape(step // 8, 8, groups * rows), axis=0)
        top = high if top is None else jnp.maximum(top, high)
    peak = jnp.max(top, axis=0, keepdims=True)
    total = None
    for start in range(0, count, step):
        part = jnp.exp2((scores[start : start + step, :] - peak) * (scale * LOG2E))
        added = jnp.sum(part.reshape(step // 8, 8, groups * rows), axis=0)
        total = added if total is None else total + added
    found = peak * scale + jnp.log(jnp.sum(total, axis=0, keepdims=True))
    first = pl.program_id(0) * groups

    @pl.when(first == 0)
    def _():
        out_ref[...] = jnp.zeros_like(out_ref)

    for group in range(groups):
        out_ref[pl.ds(first + group, 1), :rows] = found[:, group * rows : (group + 1) * rows]


def listed_scores(rows, asked_ref, prefixes_ref, tails_ref, parts_ref, out_ref):
    shard_rows, head = tails_ref.shape[0], prefixes_ref.shape[1]
    full = head + tails_ref.shape[1]
    z, y, core = lax.axis_index("z"), lax.axis_index("y"), lax.axis_index("core")
    ys, cores = lax.axis_size("y"), lax.axis_size("core")
    start = pl.multiple_of((core * ys + y) * shard_rows, shard_rows)
    dims = (((1,), (1,)), ((), ()))
    scores = lax.dot_general(
        asked_ref[:, :head], prefixes_ref[pl.ds(start, shard_rows), :], dims, preferred_element_type=jnp.float32
    ) + lax.dot_general(asked_ref[:, head:full], tails_ref[...], dims, preferred_element_type=jnp.float32)
    count = asked_ref.shape[0]
    shards = asked_ref[:, full : full + LANES].astype(jnp.float32)
    offsets = asked_ref[:, full + LANES : full + 2 * LANES].astype(jnp.float32)
    lanes = lax.broadcasted_iota(jnp.int32, (count, LANES), 1)
    mine = shards == ((z * ys + y) * cores + core).astype(jnp.float32)
    key = lanes.astype(jnp.float32) * shard_rows + offsets
    low = jnp.min(jnp.where(mine, key, float(LANES * shard_rows)), axis=1, keepdims=True)
    high = jnp.max(jnp.where(mine, key, 0.0), axis=1, keepdims=True)
    column = lax.broadcasted_iota(jnp.int32, scores.shape, 1)

    def pick(at):
        at = (at - jnp.floor(at * (1.0 / shard_rows)) * shard_rows).astype(jnp.int32)
        return jnp.sum(jnp.where(column == at, scores, 0.0), axis=1, keepdims=True)

    depth = parts_ref.shape[0]
    parts = jnp.concatenate([parts_ref[...]] * (count // depth), axis=0)
    out_ref[...] = jnp.where(lanes < rows, parts, jnp.where(lanes == rows, pick(low), pick(high)))


def finish(scale, rows, depth, row_ref, second_ref, back_ref, prev_ref, lse_ref, rerank_ref):
    count = rerank_ref.shape[1]
    cores = lax.axis_size("core")
    ring = (lax.axis_index("z") + lax.axis_index("core")) % cores
    start = pl.multiple_of((ring * lax.axis_size("y") + lax.axis_index("y")) * depth, depth)
    parts = back_ref[pl.ds(start, depth), :rows]
    peak = jnp.max(parts, axis=0, keepdims=True)
    lse_ref[...] = peak + jnp.log(jnp.sum(jnp.exp(parts - peak), axis=0, keepdims=True))
    turned = back_ref[...].T
    shape = (8, LANES)
    at = jnp.broadcast_to(row_ref[...], shape)
    low = jnp.take_along_axis(jnp.broadcast_to(turned[rows : rows + 1, :], shape), at, axis=1)
    high = jnp.take_along_axis(jnp.broadcast_to(turned[rows + 1 : rows + 2, :], shape), at, axis=1)
    values = jnp.where(second_ref[...] > 0, high[:1], low[:1])
    rerank_ref[...] = values[:, :count] * scale - prev_ref[0]


def local(prefixes, tails, queries_now, queries_prev, candidates, lse_prev):
    vmem, smem = pl.BlockSpec(memory_space=pltpu.VMEM), pl.BlockSpec(memory_space=pltpu.SMEM)
    depth, ys, cores = lax.axis_size("z"), lax.axis_size("y"), lax.axis_size("core")
    own_rows, head = queries_now.shape
    shard_rows = tails.shape[0]
    full_width = queries_prev.shape[1]
    plane = ys * cores
    turn = depth // 2
    around = [(i + turn) % depth for i in range(depth)]

    ids = candidates.reshape(-1)
    count = ids.shape[0]
    shard, offset = ids // shard_rows, ids % shard_rows
    listed = jnp.concatenate(
        [jnp.pad(shard, (0, LANES - count), constant_values=-1), jnp.pad(offset, (0, LANES - count))]
    ).astype(queries_prev.dtype)

    passages = lax.all_to_all(
        jnp.broadcast_to(prefixes[None], (plane * lax.axis_size("x"),) + prefixes.shape),
        PLANE, 0, 0, tiled=True,
    ).reshape(-1, head)

    extra = full_width // head + 1
    sent = jnp.concatenate(
        [
            queries_now.reshape(-1, 16, head),
            jnp.concatenate(
                [
                    queries_prev.reshape(extra - 1, head),
                    listed.reshape(1, head),
                    jnp.zeros((-extra % 16, head), queries_now.dtype),
                ]
            ).reshape(-1, 16, head),
        ]
    )
    orders = [around, around[::-1]]
    rings = [[z * cores + (z + ring) % cores for z in orders[ring]] for ring in range(cores)]
    column = lax.all_gather(sent, PAIR, tiled=True, axis_index_groups=rings).reshape(depth, -1, head)
    asked = column[:, own_rows : own_rows + extra].reshape(depth, extra * head)

    asked = jnp.broadcast_to(asked[None], (ys,) + asked.shape)
    asked, passages = lax.optimization_barrier((asked, passages))
    asked = lax.all_to_all(asked, "y", 0, 0, tiled=True).reshape(-1, extra * head)
    pairs = [[z * cores + (z + ring) % cores for ring in range(cores)] for z in range(depth)]
    asked = lax.all_gather(asked, PAIR, tiled=True, axis_index_groups=pairs)

    step = 4
    parts = pl.pallas_call(
        lambda *refs: partial_lse(head**-0.5, own_rows, *refs),
        grid=(depth // step,),
        in_specs=[
            pl.BlockSpec((step,) + column.shape[1:], lambda i: (i, 0, 0)),
            pl.BlockSpec(passages.shape, lambda i: (0, 0)),
        ],
        out_specs=pl.BlockSpec((depth, LANES), lambda i: (0, 0)),
        out_shape=jax.ShapeDtypeStruct((depth, LANES), jnp.float32),
        scratch_shapes=[pltpu.VMEM((passages.shape[0], step * own_rows), jnp.float32)],
        compiler_params=pltpu.CompilerParams(vmem_limit_bytes=32 * 2**20),
        cost_estimate=pl.CostEstimate(flops=2 * 2**28, bytes_accessed=2 * 2**20, transcendentals=2**21),
        name="partial_lse",
    )(column, passages)

    z, y, core = lax.axis_index("z"), lax.axis_index("y"), lax.axis_index("core")
    merged = pl.pallas_call(
        lambda *refs: listed_scores(own_rows, *refs),
        in_specs=[vmem, vmem, vmem, vmem],
        out_specs=vmem,
        out_shape=jax.ShapeDtypeStruct((plane * depth, LANES), jnp.float32),
        compiler_params=pltpu.CompilerParams(vmem_limit_bytes=32 * 2**20),
        cost_estimate=pl.CostEstimate(flops=2 * 128 * 256 * 3072, bytes_accessed=3 * 2**20, transcendentals=0),
        name="listed_scores",
    )(asked, passages, tails, parts)

    groups = [z * plane + i * cores + (z + ring) % cores for ring in range(cores) for i in range(ys) for z in orders[ring]]
    back = lax.all_to_all(merged, BACK, 0, 0, tiled=True, axis_index_groups=[groups])

    far = shard // plane
    ring, at = (shard + far) % cores, (far + turn) % depth
    row = (ring * ys + shard // cores % ys) * depth + jnp.where(ring == 0, at, depth - 1 - at)
    before = jnp.arange(count)[:, None] > jnp.arange(count)[None, :]
    second = jnp.any((shard[:, None] == shard[None, :]) & before, axis=1).astype(jnp.int32)
    lse_now, rerank = pl.pallas_call(
        lambda *refs: finish(full_width**-0.5, own_rows, depth, *refs),
        in_specs=[vmem, vmem, vmem, smem],
        out_specs=[vmem, vmem],
        out_shape=[
            jax.ShapeDtypeStruct((1, own_rows), jnp.float32),
            jax.ShapeDtypeStruct((1, count), jnp.float32),
        ],
        compiler_params=pltpu.CompilerParams(vmem_limit_bytes=32 * 2**20),
        name="finish",
    )(
        jnp.pad(row, (0, LANES - count)).reshape(1, LANES),
        jnp.pad(second, (0, LANES - count)).reshape(1, LANES),
        back,
        lse_prev,
    )
    return lse_now.reshape(-1), rerank


def solution(mesh):
    across, ways = mesh.devices.shape
    split = Mesh(mesh.devices.reshape(across // 8, 4, 2, ways), ALL)
    shard = ("z", "y", "core")
    return jax.shard_map(
        local,
        mesh=split,
        in_specs=(P(ALL, None), P(shard, None), P(ALL, None), P(ALL, None), P(ALL, None), P(ALL)),
        out_specs=(P(ALL), P(ALL, None)),
        check_vma=False,
    )
```

```python
import jax
import jax.numpy as jnp
from jax import lax
from jax.experimental import pallas as pl
from jax.experimental.pallas import tpu as pltpu
from jax.sharding import Mesh, PartitionSpec as P

ALL = ("z", "y", "core", "x")
PLANE = ("core", "y", "x")
BACK = ("z", "y", "core")
PAIR = ("z", "core")
LOG2E = 1.4426950408889634
LANES = 128


def partial_lse(scale, rows, queries_ref, passages_ref, out_ref, scores):
    groups = queries_ref.shape[0]
    width = passages_ref.shape[1]
    block = queries_ref[:, :rows, :].reshape(groups * rows, width)
    count, step = passages_ref.shape[0], 256
    top = None
    for start in range(0, count, step):
        part = lax.dot_general(
            passages_ref[start : start + step, :],
            block,
            (((1,), (1,)), ((), ())),
            preferred_element_type=jnp.float32,
        )
        scores[start : start + step, :] = part
        high = jnp.max(part.reshape(step // 8, 8, groups * rows), axis=0)
        top = high if top is None else jnp.maximum(top, high)
    peak = jnp.max(top, axis=0, keepdims=True)
    total = None
    for start in range(0, count, step):
        part = jnp.exp2((scores[start : start + step, :] - peak) * (scale * LOG2E))
        added = jnp.sum(part.reshape(step // 8, 8, groups * rows), axis=0)
        total = added if total is None else total + added
    found = peak * scale + jnp.log(jnp.sum(total, axis=0, keepdims=True))
    first = pl.program_id(0) * groups

    @pl.when(first == 0)
    def _():
        out_ref[...] = jnp.zeros_like(out_ref)

    for group in range(groups):
        out_ref[pl.ds(first + group, 1), LANES - rows :] = found[:, group * rows : (group + 1) * rows]


def listed_scores(rows, asked_ref, prefixes_ref, tails_ref, parts_ref, out_ref):
    shard_rows, head = tails_ref.shape[0], prefixes_ref.shape[1]
    full = head + tails_ref.shape[1]
    z, y, core = lax.axis_index("z"), lax.axis_index("y"), lax.axis_index("core")
    ys, cores = lax.axis_size("y"), lax.axis_size("core")
    start = pl.multiple_of((core * ys + y) * shard_rows, shard_rows)
    dims = (((1,), (1,)), ((), ()))
    scores = lax.dot_general(
        prefixes_ref[pl.ds(start, shard_rows), :], asked_ref[:, :head], dims, preferred_element_type=jnp.float32
    ) + lax.dot_general(tails_ref[...], asked_ref[:, head:full], dims, preferred_element_type=jnp.float32)
    count, depth = asked_ref.shape[0], parts_ref.shape[0]
    shards = asked_ref[:, full : full + LANES].astype(jnp.float32).T
    offsets = asked_ref[:, full + LANES : full + 2 * LANES].astype(jnp.float32).T
    mine = shards == ((z * ys + y) * cores + core).astype(jnp.float32)
    key = lax.broadcasted_iota(jnp.int32, shards.shape, 0).astype(jnp.float32) * shard_rows + offsets
    low = jnp.min(jnp.where(mine, key, float(LANES * shard_rows)), axis=0, keepdims=True)
    high = jnp.max(jnp.where(mine, key, 0.0), axis=0, keepdims=True)
    row = lax.broadcasted_iota(jnp.int32, scores.shape, 0)

    def pick(at):
        at = (at - jnp.floor(at * (1.0 / shard_rows)) * shard_rows).astype(jnp.int32)
        return jnp.sum(jnp.where(row == at, scores, 0.0), axis=0, keepdims=True)

    slots = lax.broadcasted_iota(jnp.int32, (8, count), 0)
    values = jnp.where(slots == 0, pick(low), jnp.where(slots == 1, pick(high), 0.0))
    values = jnp.concatenate([values, jnp.zeros((LANES - 8, count), jnp.float32)], axis=0).T
    lanes = lax.broadcasted_iota(jnp.int32, (count, LANES), 1)
    out_ref[...] = jnp.where(lanes < 8, values, jnp.concatenate([parts_ref[...]] * (count // depth), axis=0))


def finish(scale, rows, depth, row_ref, second_ref, back_ref, prev_ref, lse_ref, rerank_ref):
    count = rerank_ref.shape[1]
    cores = lax.axis_size("core")
    ring = (lax.axis_index("z") + lax.axis_index("core")) % cores
    start = pl.multiple_of((ring * lax.axis_size("y") + lax.axis_index("y")) * depth, depth)
    parts = back_ref[pl.ds(start, depth), LANES - rows :]
    peak = jnp.max(parts, axis=0, keepdims=True)
    lse_ref[...] = peak + jnp.log(jnp.sum(jnp.exp(parts - peak), axis=0, keepdims=True))
    turned = back_ref[...].T
    shape = (8, LANES)
    at = jnp.broadcast_to(row_ref[...], shape)
    low = jnp.take_along_axis(jnp.broadcast_to(turned[:1, :], shape), at, axis=1)
    high = jnp.take_along_axis(jnp.broadcast_to(turned[1:2, :], shape), at, axis=1)
    values = jnp.where(second_ref[...] > 0, high[:1], low[:1])
    rerank_ref[...] = values[:, :count] * scale - prev_ref[...]


def local(prefixes, tails, queries_now, queries_prev, candidates, lse_prev):
    vmem, smem = pl.BlockSpec(memory_space=pltpu.VMEM), pl.BlockSpec(memory_space=pltpu.SMEM)
    depth, ys, cores = lax.axis_size("z"), lax.axis_size("y"), lax.axis_size("core")
    own_rows, head = queries_now.shape
    shard_rows = tails.shape[0]
    full_width = queries_prev.shape[1]
    plane = ys * cores
    turn = depth // 2
    around = [(i + turn) % depth for i in range(depth)]

    ids = candidates.reshape(-1)
    count = ids.shape[0]
    shard, offset = ids // shard_rows, ids % shard_rows
    listed = jnp.concatenate(
        [jnp.pad(shard, (0, LANES - count), constant_values=-1), jnp.pad(offset, (0, LANES - count))]
    ).astype(queries_prev.dtype)

    passages = lax.all_to_all(
        jnp.broadcast_to(prefixes[None], (plane * lax.axis_size("x"),) + prefixes.shape),
        PLANE, 0, 0, tiled=True,
    ).reshape(-1, head)

    extra = full_width // head + 1
    asking = jnp.concatenate(
        [queries_prev.reshape(extra - 1, head), listed.reshape(1, head), jnp.zeros((-extra % 16, head), queries_now.dtype)]
    )
    sent = jnp.concatenate([queries_now.reshape(-1, 16, head), asking.reshape(-1, 16, head)])
    orders = [around, around[::-1]]
    rings = [[z * cores + (z + ring) % cores for z in orders[ring]] for ring in range(cores)]
    column = lax.all_gather(sent, PAIR, tiled=True, axis_index_groups=rings).reshape(depth, -1, head)
    asked = column[:, own_rows : own_rows + extra].reshape(depth, extra * head)

    asked = jnp.broadcast_to(asked[None], (ys,) + asked.shape)
    asked, passages = lax.optimization_barrier((asked, passages))
    asked = lax.all_to_all(asked, "y", 0, 0, tiled=True).reshape(-1, extra * head)
    pairs = [[z * cores + (z + ring) % cores for ring in range(cores)] for z in range(depth)]
    asked = lax.all_gather(asked, PAIR, tiled=True, axis_index_groups=pairs)

    step = 4
    parts = pl.pallas_call(
        lambda *refs: partial_lse(head**-0.5, own_rows, *refs),
        grid=(depth // step,),
        in_specs=[
            pl.BlockSpec((step,) + column.shape[1:], lambda i: (i, 0, 0)),
            pl.BlockSpec(passages.shape, lambda i: (0, 0)),
        ],
        out_specs=pl.BlockSpec((depth, LANES), lambda i: (0, 0)),
        out_shape=jax.ShapeDtypeStruct((depth, LANES), jnp.float32),
        scratch_shapes=[pltpu.VMEM((passages.shape[0], step * own_rows), jnp.float32)],
        compiler_params=pltpu.CompilerParams(vmem_limit_bytes=12 * 2**20),
        cost_estimate=pl.CostEstimate(flops=2 * 2**28, bytes_accessed=2 * 2**20, transcendentals=2**21),
        name="partial_lse",
    )(column, passages)

    z, y, core = lax.axis_index("z"), lax.axis_index("y"), lax.axis_index("core")
    merged = pl.pallas_call(
        lambda *refs: listed_scores(own_rows, *refs),
        in_specs=[vmem, vmem, vmem, vmem],
        out_specs=vmem,
        out_shape=jax.ShapeDtypeStruct((plane * depth, LANES), jnp.float32),
        compiler_params=pltpu.CompilerParams(vmem_limit_bytes=12 * 2**20),
        cost_estimate=pl.CostEstimate(flops=2 * 128 * 256 * 3072, bytes_accessed=3 * 2**20, transcendentals=0),
        name="listed_scores",
    )(asked, passages, tails, parts)

    groups = [z * plane + i * cores + (z + ring) % cores for ring in range(cores) for i in range(ys) for z in orders[ring]]
    back = lax.all_to_all(merged, BACK, 0, 0, tiled=True, axis_index_groups=[groups])

    far = shard // plane
    ring, at = (shard + far) % cores, (far + turn) % depth
    row = (ring * ys + shard // cores % ys) * depth + jnp.where(ring == 0, at, depth - 1 - at)
    before = jnp.arange(count)[:, None] > jnp.arange(count)[None, :]
    second = jnp.any((shard[:, None] == shard[None, :]) & before, axis=1).astype(jnp.int32)
    lse_now, rerank = pl.pallas_call(
        lambda *refs: finish(full_width**-0.5, own_rows, depth, *refs),
        in_specs=[vmem, vmem, vmem, vmem],
        out_specs=[vmem, vmem],
        out_shape=[
            jax.ShapeDtypeStruct((1, own_rows), jnp.float32),
            jax.ShapeDtypeStruct((1, count), jnp.float32),
        ],
        compiler_params=pltpu.CompilerParams(vmem_limit_bytes=12 * 2**20),
        name="finish",
    )(
        jnp.pad(row, (0, LANES - count)).reshape(1, LANES),
        jnp.pad(second, (0, LANES - count)).reshape(1, LANES),
        back,
        lse_prev.reshape(1, 1),
    )
    return lse_now.reshape(-1), rerank


def solution(mesh):
    across, ways = mesh.devices.shape
    split = Mesh(mesh.devices.reshape(across // 8, 4, 2, ways), ALL)
    shard = ("z", "y", "core")
    return jax.shard_map(
        local,
        mesh=split,
        in_specs=(P(ALL, None), P(shard, None), P(ALL, None), P(ALL, None), P(ALL, None), P(ALL)),
        out_specs=(P(ALL), P(ALL, None)),
        check_vma=False,
    )
```

```python
import jax
import jax.numpy as jnp
from jax import lax
from jax.experimental import pallas as pl
from jax.experimental.pallas import tpu as pltpu
from jax.sharding import Mesh, PartitionSpec as P

ALL = ("z", "y", "core", "x")
PLANE = ("core", "y", "x")
BACK = ("z", "y", "core")
PAIR = ("z", "core")
LOG2E = 1.4426950408889634
LANES = 128


def partial_lse(scale, rows, queries_ref, passages_ref, out_ref, scores):
    groups = queries_ref.shape[0]
    width = passages_ref.shape[1]
    block = queries_ref[:, :rows, :].reshape(groups * rows, width)
    count, step = passages_ref.shape[0], 256
    top = None
    for start in range(0, count, step):
        part = lax.dot_general(
            passages_ref[start : start + step, :],
            block,
            (((1,), (1,)), ((), ())),
            preferred_element_type=jnp.float32,
        )
        scores[start : start + step, :] = part
        high = jnp.max(part.reshape(step // 8, 8, groups * rows), axis=0)
        top = high if top is None else jnp.maximum(top, high)
    peak = jnp.max(top, axis=0, keepdims=True)
    total = None
    for start in range(0, count, step):
        part = jnp.exp2((scores[start : start + step, :] - peak) * (scale * LOG2E))
        added = jnp.sum(part.reshape(step // 8, 8, groups * rows), axis=0)
        total = added if total is None else total + added
    found = peak * scale + jnp.log(jnp.sum(total, axis=0, keepdims=True))
    first = pl.program_id(0) * groups

    @pl.when(first == 0)
    def _():
        out_ref[...] = jnp.zeros_like(out_ref)

    for group in range(groups):
        out_ref[pl.ds(first + group, 1), :rows] = found[:, group * rows : (group + 1) * rows]


def listed_scores(rows, asked_ref, prefixes_ref, tails_ref, parts_ref, out_ref):
    shard_rows, head = tails_ref.shape[0], prefixes_ref.shape[1]
    full = head + tails_ref.shape[1]
    z, y, core = lax.axis_index("z"), lax.axis_index("y"), lax.axis_index("core")
    ys, cores = lax.axis_size("y"), lax.axis_size("core")
    start = pl.multiple_of((core * ys + y) * shard_rows, shard_rows)
    dims = (((1,), (1,)), ((), ()))
    scores = lax.dot_general(
        asked_ref[:, :head], prefixes_ref[pl.ds(start, shard_rows), :], dims, preferred_element_type=jnp.float32
    ) + lax.dot_general(asked_ref[:, head:full], tails_ref[...], dims, preferred_element_type=jnp.float32)
    count = asked_ref.shape[0]
    shards = asked_ref[:, full : full + LANES].astype(jnp.float32)
    offsets = asked_ref[:, full + LANES : full + 2 * LANES].astype(jnp.float32)
    lanes = lax.broadcasted_iota(jnp.int32, (count, LANES), 1)
    mine = shards == ((z * ys + y) * cores + core).astype(jnp.float32)
    key = lanes.astype(jnp.float32) * shard_rows + offsets
    low = jnp.min(jnp.where(mine, key, float(LANES * shard_rows)), axis=1, keepdims=True)
    high = jnp.max(jnp.where(mine, key, 0.0), axis=1, keepdims=True)
    column = lax.broadcasted_iota(jnp.int32, scores.shape, 1)

    def pick(at):
        at = (at - jnp.floor(at * (1.0 / shard_rows)) * shard_rows).astype(jnp.int32)
        return jnp.sum(jnp.where(column == at, scores, 0.0), axis=1, keepdims=True)

    depth = parts_ref.shape[0]
    parts = jnp.concatenate([parts_ref[...]] * (count // depth), axis=0)
    out_ref[...] = jnp.where(lanes < rows, parts, jnp.where(lanes == rows, pick(low), pick(high)))


def finish(scale, rows, depth, row_ref, second_ref, back_ref, prev_ref, lse_ref, rerank_ref):
    count = rerank_ref.shape[1]
    cores = lax.axis_size("core")
    ring = (lax.axis_index("z") + lax.axis_index("core")) % cores
    start = pl.multiple_of((ring * lax.axis_size("y") + lax.axis_index("y")) * depth, depth)
    parts = back_ref[pl.ds(start, depth), :rows]
    peak = jnp.max(parts, axis=0, keepdims=True)
    lse_ref[...] = peak + jnp.log(jnp.sum(jnp.exp(parts - peak), axis=0, keepdims=True))
    turned = back_ref[...].T
    shape = (8, LANES)
    at = jnp.broadcast_to(row_ref[...], shape)
    low = jnp.take_along_axis(jnp.broadcast_to(turned[rows : rows + 1, :], shape), at, axis=1)
    high = jnp.take_along_axis(jnp.broadcast_to(turned[rows + 1 : rows + 2, :], shape), at, axis=1)
    values = jnp.where(second_ref[...] > 0, high[:1], low[:1])
    rerank_ref[...] = values[:, :count] * scale - prev_ref[0]


def local(prefixes, tails, queries_now, queries_prev, candidates, lse_prev):
    vmem, smem = pl.BlockSpec(memory_space=pltpu.VMEM), pl.BlockSpec(memory_space=pltpu.SMEM)
    depth, ys, cores = lax.axis_size("z"), lax.axis_size("y"), lax.axis_size("core")
    own_rows, head = queries_now.shape
    shard_rows = tails.shape[0]
    full_width = queries_prev.shape[1]
    plane = ys * cores
    turn = 5 * depth // 8
    around = [(i + turn) % depth for i in range(depth)]

    ids = candidates.reshape(-1)
    count = ids.shape[0]
    shard, offset = ids // shard_rows, ids % shard_rows
    listed = jnp.concatenate(
        [jnp.pad(shard, (0, LANES - count), constant_values=-1), jnp.pad(offset, (0, LANES - count))]
    ).astype(queries_prev.dtype)

    passages = lax.all_to_all(
        jnp.broadcast_to(prefixes[None], (plane * lax.axis_size("x"),) + prefixes.shape),
        PLANE, 0, 0, tiled=True,
    ).reshape(-1, head)

    extra = full_width // head + 1
    sent = jnp.concatenate(
        [
            queries_now,
            queries_prev.reshape(extra - 1, head),
            listed.reshape(1, head),
            jnp.zeros((-extra % 16, head), queries_now.dtype),
        ]
    )
    orders = [around, around[::-1]]
    rings = [[z * cores + (z + ring) % cores for z in orders[ring]] for ring in range(cores)]
    column = lax.all_gather(sent, PAIR, axis_index_groups=rings)
    asked = column[:, own_rows : own_rows + extra].reshape(depth, extra * head)

    asked = jnp.broadcast_to(asked[None], (ys,) + asked.shape)
    asked, passages = lax.optimization_barrier((asked, passages))
    asked = lax.all_to_all(asked, "y", 0, 0, tiled=True).reshape(-1, extra * head)
    pairs = [[z * cores + (z + ring) % cores for ring in range(cores)] for z in range(depth)]
    asked = lax.all_gather(asked, PAIR, tiled=True, axis_index_groups=pairs)

    step = 4
    parts = pl.pallas_call(
        lambda *refs: partial_lse(head**-0.5, own_rows, *refs),
        grid=(depth // step,),
        in_specs=[
            pl.BlockSpec((step,) + column.shape[1:], lambda i: (i, 0, 0)),
            pl.BlockSpec(passages.shape, lambda i: (0, 0)),
        ],
        out_specs=pl.BlockSpec((depth, LANES), lambda i: (0, 0)),
        out_shape=jax.ShapeDtypeStruct((depth, LANES), jnp.float32),
        scratch_shapes=[pltpu.VMEM((passages.shape[0], step * own_rows), jnp.float32)],
        compiler_params=pltpu.CompilerParams(vmem_limit_bytes=32 * 2**20),
        cost_estimate=pl.CostEstimate(flops=2 * 2**28, bytes_accessed=2 * 2**20, transcendentals=2**21),
        name="partial_lse",
    )(column, passages)

    z, y, core = lax.axis_index("z"), lax.axis_index("y"), lax.axis_index("core")
    merged = pl.pallas_call(
        lambda *refs: listed_scores(own_rows, *refs),
        in_specs=[vmem, vmem, vmem, vmem],
        out_specs=vmem,
        out_shape=jax.ShapeDtypeStruct((plane * depth, LANES), jnp.float32),
        compiler_params=pltpu.CompilerParams(vmem_limit_bytes=32 * 2**20),
        cost_estimate=pl.CostEstimate(flops=2 * 128 * 256 * 3072, bytes_accessed=3 * 2**20, transcendentals=0),
        name="listed_scores",
    )(asked, passages, tails, parts)

    groups = [z * plane + i * cores + (z + ring) % cores for ring in range(cores) for i in range(ys) for z in orders[ring]]
    back = lax.all_to_all(merged, BACK, 0, 0, tiled=True, axis_index_groups=[groups])

    far = shard // plane
    ring, at = (shard + far) % cores, (far - turn) % depth
    row = (ring * ys + shard // cores % ys) * depth + jnp.where(ring == 0, at, depth - 1 - at)
    before = jnp.arange(count)[:, None] > jnp.arange(count)[None, :]
    second = jnp.any((shard[:, None] == shard[None, :]) & before, axis=1).astype(jnp.int32)
    lse_now, rerank = pl.pallas_call(
        lambda *refs: finish(full_width**-0.5, own_rows, depth, *refs),
        in_specs=[vmem, vmem, vmem, smem],
        out_specs=[vmem, vmem],
        out_shape=[
            jax.ShapeDtypeStruct((1, own_rows), jnp.float32),
            jax.ShapeDtypeStruct((1, count), jnp.float32),
        ],
        compiler_params=pltpu.CompilerParams(vmem_limit_bytes=32 * 2**20),
        name="finish",
    )(
        jnp.pad(row, (0, LANES - count)).reshape(1, LANES),
        jnp.pad(second, (0, LANES - count)).reshape(1, LANES),
        back,
        lse_prev,
    )
    return lse_now.reshape(-1), rerank


def solution(mesh):
    across, ways = mesh.devices.shape
    split = Mesh(mesh.devices.reshape(across // 8, 4, 2, ways), ALL)
    shard = ("z", "y", "core")
    return jax.shard_map(
        local,
        mesh=split,
        in_specs=(P(ALL, None), P(shard, None), P(ALL, None), P(ALL, None), P(ALL, None), P(ALL)),
        out_specs=(P(ALL), P(ALL, None)),
        check_vma=False,
    )
```
